32 devices in a mesh: group: 2 (over x), adapter: 8 (over z, y), tensor: 2 (over core).
Axes of the slice: x: 2, y: 2, z: 4, core: 2. Of those that a mesh axis runs over, the one named last changes fastest.
Arguments:
- tokens: bfloat16 [768, 8192], P(('group', 'adapter'), 'tensor'), parts along dimension 0, may hold values from -6 to 6
- token_row_adapter: int32 [768, 1], P('group'), parts along dimension 0, may hold values from 0 to 7
- output_weight: bfloat16 [8192, 8192], P('tensor', 'adapter'), may hold values from -0.0625 to 0.0625
- down_weight: bfloat16 [16, 8192, 64], P(('group', 'adapter'), 'tensor'), parts along dimension 0, may hold values from -0.0625 to 0.0625
- up_weight: bfloat16 [16, 64, 8192], P('group', 'tensor', 'adapter'), parts along dimension 0, may hold values from -0.75 to 0.75
Outputs:
- projected: bfloat16 [768, 8192], P('group', 'adapter'), parts along dimension 0
The draws below stay inside these ranges and needn't reach their ends.
There are 2 independent parts, one for each index of `group`. The reference program is written for one: setup_inputs(seed, part) draws one part's arguments, and reference() takes and returns one part's arrays. A program takes and returns all parts, laid end to end along the dimension named above; an argument that names none is the same for every part. Nothing has to cross between parts.
Inputs may be any that keep to these rules, and one draw needn't show every extreme that they name: `token_row_adapter`: each adapter is named by at least one row.
All inputs are finite; a program needn't handle non-finite values.
Results may differ from the reference program's by a relative error of at most 0.011.
Values may be sent and summed in bfloat16 or wider, within the bound.
A program may use at most 128 MiB of HBM per device.

```python
import jax
import jax.numpy as jnp
from jax import lax

MODEL_WIDTH = 8192
ADAPTER_RANK = 64
TOKENS = 384
ADAPTER_COUNT = 8


def level_of(stream_key, shape, cuts, least, largest):
    def one(position, shards_of):
        steps = jax.random.uniform(jax.random.fold_in(jax.random.fold_in(stream_key, 6), position), (shards_of,), jnp.float32, least / len(cuts), largest / len(cuts))
        return jnp.repeat(jnp.exp(steps), shape[position] // shards_of).reshape((-1,) + (1,) * (len(shape) - position - 1))

    gain = one(*cuts[0])
    for cut in cuts[1:]:
        gain = gain * one(*cut)
    return gain


def choose_distinct(key, rows, count, top, lift):
    order = jax.random.permutation(jax.random.fold_in(key, 1), count)
    pull = order
    for power in range(3):
        pull = pull * pull // count
    pull = pull * lift // count
    chance = jax.random.randint(jax.random.fold_in(key, 2), (rows, count), 0, 4096) + pull
    fixed_rows = jax.random.permutation(jax.random.fold_in(key, 3), rows)[jnp.arange(count) % rows]
    chance = jnp.where(jnp.arange(rows)[:, None] == fixed_rows[None, :], 1 << 14, chance)
    priority = chance * count + jnp.arange(count)
    return lax.top_k(priority.astype(jnp.int32), top)[1].astype(jnp.int32)


def centred(own_key, dims, deviation, most, pieces=(), kind=jnp.bfloat16):
    entries = jax.random.normal(own_key, dims, jnp.float32) * deviation
    if len(pieces) > 0:
        entries = level_of(own_key, dims, pieces, -0.22, 0.18) * entries
    return jnp.clip(entries, min=-most, max=most).astype(kind)


def setup_inputs(seed: int = 0, part: int = 0) -> dict:
    key_of = jax.random.split(jax.random.key(seed), 6)
    own_keys = jax.random.split(jax.random.fold_in(key_of[5], part), 6)
    return {
        "tokens": centred(own_keys[0], (TOKENS, MODEL_WIDTH), 1.0, 6.0, ((0, 8), (1, 2))),
        "token_row_adapter": choose_distinct(own_keys[1], TOKENS, ADAPTER_COUNT, 1, 2048),
        "output_weight": centred(key_of[2], (MODEL_WIDTH, MODEL_WIDTH), MODEL_WIDTH ** -0.5, 0.0625, ((0, 2), (1, 8))),
        "down_weight": centred(own_keys[3], (ADAPTER_COUNT, MODEL_WIDTH, ADAPTER_RANK), MODEL_WIDTH ** -0.5, 0.0625, ((0, 8), (1, 2))),
        "up_weight": centred(own_keys[4], (ADAPTER_COUNT, ADAPTER_RANK, MODEL_WIDTH), ADAPTER_RANK ** -0.5, 0.75, ((1, 2), (2, 8))),
    }


def reference(tokens, token_row_adapter, output_weight, down_weight, up_weight):
    flat_ids = token_row_adapter[:, 0]
    base = jnp.dot(tokens, output_weight, preferred_element_type=jnp.float32)

    def add_one(adapter_index, total):
        rows_projected = jnp.dot(tokens, down_weight[adapter_index], preferred_element_type=jnp.float32)
        chosen = (flat_ids == adapter_index).astype(jnp.float32)
        return total + chosen[:, None] * rows_projected

    low = lax.fori_loop(0, ADAPTER_COUNT, add_one, jnp.zeros((TOKENS, ADAPTER_RANK), jnp.float32))
    low = low.astype(jnp.bfloat16)
    onehot = (flat_ids[:, None] == jnp.arange(ADAPTER_COUNT, dtype=jnp.int32)[None, :]).astype(jnp.bfloat16)
    scattered_rows = (onehot[:, :, None] * low[:, None, :]).reshape(TOKENS, ADAPTER_COUNT * ADAPTER_RANK)
    adapter_update = jnp.dot(scattered_rows, up_weight.reshape(ADAPTER_COUNT * ADAPTER_RANK, MODEL_WIDTH), preferred_element_type=jnp.float32)
    return (base + 2.0 * adapter_update).astype(jnp.bfloat16)
```

```python
import functools

import jax
import jax.numpy as jnp
from jax import lax
from jax.experimental import pallas as pl
from jax.experimental.pallas import tpu as pltpu
from jax.sharding import PartitionSpec as P

adapter_scale = 2.0
CHUNK = 16
TILE = 256
MESH = pl.DeviceIdType.MESH


def when(condition, action):
    pl.when(condition)(action)


def kernel(
    count, wide, phases,
    x_hbm, ids_ref, w_hbm, down_hbm, up_hbm, out_ref,
    xs, w, down, up, part_out, part_in, base_out, base_in, lows,
    load_sem, own_sem,
    up_send, up_recv,
    right_send, left_send, line_recv,
    side_send, side_recv, cross_send, cross_recv,
    part_send, part_recv, base_send, base_recv, low_send, low_recv,
):
    deep = count // wide
    me = lax.axis_index("adapter")
    core = lax.axis_index("tensor")
    z, y = lax.div(me, wide), lax.rem(me, wide)
    features = x_hbm.shape[1]
    half = features // 2
    rank = down.shape[1]
    half_rank = rank // 2
    columns = w.shape[1]
    rows = count * CHUNK
    pack = rows // 2
    beside = z + 1 - 2 * lax.rem(z, 2)
    mirror = 1 - y

    def place(zz, yy):
        return zz * wide + yy

    def block(phase, a, first=0, size=features):
        return xs.at[phase, pl.ds(pl.multiple_of(a * CHUNK, CHUNK), CHUNK), pl.ds(first, size)]

    def own(phase):
        return x_hbm.at[pl.ds(phase * CHUNK, CHUNK), :]

    def remote(src, dst, send, recv, **device):
        return pltpu.make_async_remote_copy(
            src_ref=src, dst_ref=dst, send_sem=send, recv_sem=recv,
            device_id=device, device_id_type=MESH,
        )

    w_copy = pltpu.make_async_copy(w_hbm, w, load_sem.at[0])
    down_copy = pltpu.make_async_copy(down_hbm.at[0], down, load_sem.at[1])
    up_rows = pl.ds(pl.multiple_of(core * half_rank, half_rank), half_rank)
    up_copy = pltpu.make_async_copy(up_hbm, up.at[:, up_rows, :], load_sem.at[2])
    up_remote = remote(up_hbm, up.at[:, up_rows, :], up_send, up_recv, tensor=1 - core)

    def own_copy(phase):
        return pltpu.make_async_copy(own(phase), block(phase, me), own_sem.at[phase])

    w_copy.start()
    down_copy.start()
    up_copy.start()
    for phase in range(phases):
        own_copy(phase).start()

    barrier = pltpu.get_barrier_semaphore()
    pl.semaphore_signal(barrier, inc=1, device_id={"tensor": 1 - core}, device_id_type=MESH)
    for k in range(1, count):
        pl.semaphore_signal(
            barrier, inc=1, device_id={"adapter": lax.rem(me + k, count)}, device_id_type=MESH
        )
    pl.semaphore_wait(barrier, count)

    def right(phase, s, src=None):
        dst = block(phase, place(s, y))
        return remote(dst if src is None else src, dst, right_send.at[phase, s],
                      line_recv.at[phase, s], adapter=lax.rem(me + wide, count))

    def left(phase, s, src=None):
        dst = block(phase, place(s, y))
        return remote(dst if src is None else src, dst, left_send.at[phase, s],
                      line_recv.at[phase, s], adapter=lax.rem(me + count - wide, count))

    def side(phase, s, size, src=None):
        dst = block(phase, place(s, y), 0, size)
        return remote(dst if src is None else src, dst, side_send.at[phase, s],
                      side_recv.at[phase, s], adapter=place(z, mirror))

    def side_in(phase, s, size):
        dst = block(phase, place(s, mirror), 0, size)
        return remote(dst, dst, side_send.at[phase, s], side_recv.at[phase, s],
                      adapter=place(z, mirror))

    def cross(phase, s):
        dst = block(phase, place(s, mirror), half, half)
        return remote(dst, dst, cross_send.at[phase], cross_recv.at[phase],
                      adapter=place(beside, y))

    def by_size(s, action):
        when(s == beside, lambda: action(half))
        when(s != beside, lambda: action(features))

    def send_own(phase):
        when(z + 1 < deep, lambda: right(phase, z, own(phase)).start())
        when(z > 0, lambda: left(phase, z, own(phase)).start())
        if wide == 2:
            side(phase, z, features, own(phase)).start()

    def relay(phase, d):
        def pass_on(s):
            if wide == 2:
                by_size(s, lambda size: side(phase, s, size).start())

        def from_left():
            right(phase, z - d).wait_recv()
            when(z + 1 < deep, lambda: right(phase, z - d).start())
            pass_on(z - d)

        def from_right():
            left(phase, z + d).wait_recv()
            when(z > 0, lambda: left(phase, z + d).start())
            pass_on(z + d)

        when(z >= d, from_left)
        when(z + d < deep, from_right)

    def pass_across(phase):
        if wide == 2:
            side_in(phase, z, features).wait_recv()
            cross(phase, z).start()

    def finish(phase):
        own_copy(phase).wait()
        if wide == 2:
            for s in range(deep):
                when(z != s, lambda s=s: by_size(
                    s, lambda size: side_in(phase, s, size).wait_recv()))
            cross(phase, beside).wait_recv()

    def part_copy(phase):
        return remote(part_out.at[phase], part_in.at[phase], part_send.at[phase],
                      part_recv.at[phase], tensor=1 - core)

    def base_copy(phase):
        return remote(base_out.at[phase], base_in.at[phase], base_send.at[phase],
                      base_recv.at[phase], tensor=1 - core)

    def low_copy(phase, k):
        return remote(lows.at[phase, me], lows.at[phase, me], low_send.at[phase, k],
                      low_recv.at[phase, me], adapter=lax.rem(me + k, count))

    def low_in(phase, k):
        source = lax.rem(me + k, count)
        slot = lows.at[phase, source]
        return remote(slot, slot, low_send.at[phase, k], low_recv.at[phase, source],
                      adapter=source)

    def project_down(phase):
        ids = jnp.concatenate(
            [ids_ref[pl.ds((a * phases + phase) * CHUNK, CHUNK), :] for a in range(count)], axis=0
        )
        low = jnp.dot(xs[phase], down[...], preferred_element_type=jnp.float32)
        low = jnp.where(ids == me, low, 0.0)
        part_out[phase] = jnp.concatenate([low[:pack], low[pack:]], axis=1)
        part_copy(phase).start()

    def project(phase):
        @pl.loop(0, columns // TILE)
        def _(n):
            cols = pl.ds(pl.multiple_of(n * TILE, TILE), TILE)
            base_out[phase, :, cols] = jnp.dot(
                xs[phase], w[:, cols], preferred_element_type=jnp.float32
            )

        base_copy(phase).start()

    def share_low(phase):
        part_copy(phase).wait_recv()
        lows[phase, me] = (part_out[phase] + part_in[phase]).astype(jnp.bfloat16)
        for k in range(1, count):
            low_copy(phase, k).start()

    def write(phase):
        for k in range(1, count):
            low_in(phase, k).wait_recv()
        base_copy(phase).wait_recv()
        top = jnp.concatenate([lows[phase, a, :, :rank] for a in range(count)], axis=1)
        low_half = jnp.concatenate([lows[phase, a, :, rank:] for a in range(count)], axis=1)
        scattered = jnp.concatenate([top, low_half], axis=0)
        for n in range(columns // TILE):
            cols = pl.ds(n * TILE, TILE)
            delta = jnp.dot(
                scattered, up[:, :, cols].reshape(count * rank, TILE),
                preferred_element_type=jnp.float32,
            )
            total = base_out[phase, :, cols] + base_in[phase, :, cols] + adapter_scale * delta
            total = total.astype(jnp.bfloat16)
            for a in range(count):
                out_ref[pl.ds((a * phases + phase) * CHUNK, CHUNK), cols] = (
                    total[a * CHUNK:(a + 1) * CHUNK]
                )

    send_own(0)
    up_remote.start()
    for phase in range(phases):
        relay(phase, 1)
        pass_across(phase)
        if phase + 1 < phases:
            send_own(phase + 1)
        if phase == 1:
            down_copy.wait()
            w_copy.wait()
        if phase >= 1:
            project_down(phase - 1)
            project(phase - 1)
        for d in range(2, deep):
            relay(phase, d)
            if d == 2 and phase >= 1:
                share_low(phase - 1)
        finish(phase)
    if phases == 1:
        down_copy.wait()
        w_copy.wait()
    last = phases - 1
    project_down(last)
    up_copy.wait()
    up_remote.wait_recv()
    project(last)
    share_low(last)
    for phase in range(phases):
        write(phase)

    up_remote.wait_send()
    for phase in range(phases):
        part_copy(phase).wait_send()
        base_copy(phase).wait_send()
        for k in range(1, count):
            low_copy(phase, k).wait_send()
        for s in range(deep):
            when(jnp.logical_and(z >= s, z + 1 < deep),
                 lambda s=s: right(phase, s).wait_send())
            when(jnp.logical_and(z <= s, z > 0),
                 lambda s=s: left(phase, s).wait_send())
            if wide == 2:
                by_size(s, lambda size, s=s: side(phase, s, size).wait_send())
        if wide == 2:
            cross(phase, z).wait_send()


def local(count, wide, tokens, token_row_adapter, output_weight, down_weight, up_weight):
    own_rows, features = tokens.shape
    total_rows = token_row_adapter.shape[0]
    columns = output_weight.shape[1]
    rank = down_weight.shape[2]
    phases = own_rows // CHUNK
    deep = count // wide
    rows = count * CHUNK
    dma = pltpu.SemaphoreType.DMA
    anywhere = pl.BlockSpec(memory_space=pl.ANY)
    vmem = pl.BlockSpec(memory_space=pltpu.VMEM)
    return pl.pallas_call(
        functools.partial(kernel, count, wide, phases),
        out_shape=jax.ShapeDtypeStruct((total_rows, columns), jnp.bfloat16),
        in_specs=[anywhere, vmem, anywhere, anywhere, anywhere],
        out_specs=vmem,
        scratch_shapes=[
            pltpu.VMEM((phases, rows, features), jnp.bfloat16),
            pltpu.VMEM((features, columns), jnp.bfloat16),
            pltpu.VMEM((features, rank), jnp.bfloat16),
            pltpu.VMEM((count, rank, columns), jnp.bfloat16),
            pltpu.VMEM((phases, rows // 2, 2 * rank), jnp.float32),
            pltpu.VMEM((phases, rows // 2, 2 * rank), jnp.float32),
            pltpu.VMEM((phases, rows, columns), jnp.float32),
            pltpu.VMEM((phases, rows, columns), jnp.float32),
            pltpu.VMEM((phases, count, rows // 2, 2 * rank), jnp.bfloat16),
            dma((3,)), dma((phases,)),
            dma, dma,
            dma((phases, deep)), dma((phases, deep)), dma((phases, deep)),
            dma((phases, deep)), dma((phases, deep)), dma((phases,)), dma((phases,)),
            dma((phases,)), dma((phases,)), dma((phases,)), dma((phases,)),
            dma((phases, count)), dma((phases, count)),
        ],
        compiler_params=pltpu.CompilerParams(
            collective_id=0, has_side_effects=True, vmem_limit_bytes=48 << 20
        ),
    )(tokens, token_row_adapter, output_weight, down_weight, up_weight)


def solution(mesh):
    count = mesh.shape["adapter"]
    wide = 2 if count == 8 else 1
    placed = (
        P(("group", "adapter"), "tensor"),
        P("group", None),
        P("tensor", "adapter"),
        P(("group", "adapter"), "tensor", None),
        P("group", "tensor", "adapter"),
    )
    return jax.shard_map(
        functools.partial(local, count, wide),
        mesh=mesh, in_specs=placed, out_specs=P("group", "adapter"), check_vma=False,
    )
```

```python
import functools

import jax
import jax.numpy as jnp
from jax import lax
from jax.experimental import pallas as pl
from jax.experimental.pallas import tpu as pltpu
from jax.sharding import PartitionSpec as P

adapter_scale = 2.0
CHUNK = 16
TILE = 256
MESH = pl.DeviceIdType.MESH


def when(condition, action):
    pl.when(condition)(action)


def kernel(
    count, wide, phases,
    x_hbm, ids_ref, w_hbm, down_hbm, up_hbm, out_ref,
    xs, w, down, up, part_out, part_in, base_out, base_in, pair, lows,
    load_sem, own_sem,
    up_send, up_recv,
    right_send, left_send, line_recv,
    side_send, side_recv, cross_send, cross_recv,
    part_send, part_recv, base_send, base_recv, pair_send, pair_recv, low_send, low_recv,
):
    deep = count // wide
    me = lax.axis_index("adapter")
    core = lax.axis_index("tensor")
    z, y = lax.div(me, wide), lax.rem(me, wide)
    features = x_hbm.shape[1]
    half = features // 2
    rank = down.shape[0]
    half_rank = rank // 2
    columns = w.shape[1]
    rows = count * CHUNK
    beside = z + 1 - 2 * lax.rem(z, 2)
    mirror = 1 - y

    def place(zz, yy):
        return zz * wide + yy

    def block(phase, a, first=0, size=features):
        return xs.at[phase, pl.ds(pl.multiple_of(a * CHUNK, CHUNK), CHUNK), pl.ds(first, size)]

    def own(phase):
        return x_hbm.at[pl.ds(phase * CHUNK, CHUNK), :]

    def remote(src, dst, send, recv, **device):
        return pltpu.make_async_remote_copy(
            src_ref=src, dst_ref=dst, send_sem=send, recv_sem=recv,
            device_id=device, device_id_type=MESH,
        )

    w_copy = pltpu.make_async_copy(w_hbm, w, load_sem.at[0])
    down_copy = pltpu.make_async_copy(down_hbm.at[0], down, load_sem.at[1])
    up_rows = pl.ds(pl.multiple_of(core * half_rank, half_rank), half_rank)
    up_copy = pltpu.make_async_copy(up_hbm, up.at[:, up_rows, :], load_sem.at[2])
    up_remote = remote(up_hbm, up.at[:, up_rows, :], up_send, up_recv, tensor=1 - core)

    def own_copy(phase):
        return pltpu.make_async_copy(own(phase), block(phase, me), own_sem.at[phase])

    w_copy.start()
    down_copy.start()
    up_copy.start()
    for phase in range(phases):
        own_copy(phase).start()

    barrier = pltpu.get_barrier_semaphore()
    pl.semaphore_signal(barrier, inc=1, device_id={"tensor": 1 - core}, device_id_type=MESH)
    for k in range(1, deep):
        pl.semaphore_signal(
            barrier, inc=1, device_id={"adapter": lax.rem(me + k * wide, count)},
            device_id_type=MESH,
        )
    if wide == 2:
        pl.semaphore_signal(
            barrier, inc=1, device_id={"adapter": place(z, mirror)}, device_id_type=MESH
        )
    pl.semaphore_wait(barrier, deep - 1 + wide)

    def right(phase, s, src=None):
        dst = block(phase, place(s, y))
        return remote(dst if src is None else src, dst, right_send.at[phase, s],
                      line_recv.at[phase, s], adapter=lax.rem(me + wide, count))

    def left(phase, s, src=None):
        dst = block(phase, place(s, y))
        return remote(dst if src is None else src, dst, left_send.at[phase, s],
                      line_recv.at[phase, s], adapter=lax.rem(me + count - wide, count))

    def side(phase, s, size, src=None):
        dst = block(phase, place(s, y), 0, size)
        return remote(dst if src is None else src, dst, side_send.at[phase, s],
                      side_recv.at[phase, s], adapter=place(z, mirror))

    def side_in(phase, s, size):
        dst = block(phase, place(s, mirror), 0, size)
        return remote(dst, dst, side_send.at[phase, s], side_recv.at[phase, s],
                      adapter=place(z, mirror))

    def cross(phase, s):
        dst = block(phase, place(s, mirror), half, half)
        return remote(dst, dst, cross_send.at[phase], cross_recv.at[phase],
                      adapter=place(beside, y))

    def by_size(s, action):
        when(s == beside, lambda: action(half))
        when(s != beside, lambda: action(features))

    def send_own(phase):
        when(z + 1 < deep, lambda: right(phase, z, own(phase)).start())
        when(z > 0, lambda: left(phase, z, own(phase)).start())
        if wide == 2:
            side(phase, z, features, own(phase)).start()

    def relay(phase, d):
        def pass_on(s):
            if wide == 2:
                by_size(s, lambda size: side(phase, s, size).start())

        def from_left():
            right(phase, z - d).wait_recv()
            when(z + 1 < deep, lambda: right(phase, z - d).start())
            pass_on(z - d)

        def from_right():
            left(phase, z + d).wait_recv()
            when(z > 0, lambda: left(phase, z + d).start())
            pass_on(z + d)

        when(z >= d, from_left)
        when(z + d < deep, from_right)

    def pass_across(phase):
        if wide == 2:
            side_in(phase, z, features).wait_recv()
            cross(phase, z).start()

    def finish(phase):
        own_copy(phase).wait()
        if wide == 2:
            for s in range(deep):
                when(z != s, lambda s=s: by_size(
                    s, lambda size: side_in(phase, s, size).wait_recv()))
            cross(phase, beside).wait_recv()

    def part_copy(phase):
        return remote(part_out.at[phase], part_in.at[phase], part_send.at[phase],
                      part_recv.at[phase], tensor=1 - core)

    def base_copy(phase):
        return remote(base_out.at[phase], base_in.at[phase], base_send.at[phase],
                      base_recv.at[phase], tensor=1 - core)

    def pair_copy(phase):
        return remote(pair.at[phase, 0], pair.at[phase, 1], pair_send.at[phase],
                      pair_recv.at[phase], adapter=place(z, mirror))

    def low_copy(phase, k):
        return remote(lows.at[phase, z], lows.at[phase, z], low_send.at[phase, k],
                      low_recv.at[phase, z], adapter=lax.rem(me + k * wide, count))

    def low_in(phase, k):
        source = lax.rem(z + k, deep)
        slot = lows.at[phase, source]
        return remote(slot, slot, low_send.at[phase, k], low_recv.at[phase, source],
                      adapter=place(source, y))

    def phase_ids(phase):
        return jnp.concatenate(
            [ids_ref[:, pl.ds((a * phases + phase) * CHUNK, CHUNK)] for a in range(count)], axis=1
        )

    def project_down(phase):
        low = lax.dot_general(
            down[...], xs[phase], (((1,), (1,)), ((), ())), preferred_element_type=jnp.float32
        )
        part_out[phase] = jnp.where(phase_ids(phase) == me, low, 0.0)
        part_copy(phase).start()

    def project(phase):
        @pl.loop(0, columns // TILE)
        def _(n):
            cols = pl.ds(pl.multiple_of(n * TILE, TILE), TILE)
            base_out[phase, :, cols] = jnp.dot(
                xs[phase], w[:, cols], preferred_element_type=jnp.float32
            )

        base_copy(phase).start()

    def share_low(phase):
        part_copy(phase).wait_recv()
        low = (part_out[phase] + part_in[phase]).astype(jnp.bfloat16)
        if wide == 2:
            pair[phase, 0] = low
            pair_copy(phase).start()
        else:
            lows[phase, z] = low

    def spread_low(phase):
        if wide == 2:
            pair_copy(phase).wait_recv()
            lows[phase, z] = pair[phase, 0] + pair[phase, 1]
        for k in range(1, deep):
            low_copy(phase, k).start()

    def write(phase):
        for k in range(1, deep):
            low_in(phase, k).wait_recv()
        base_copy(phase).wait_recv()
        low = lows[phase, 0].astype(jnp.float32)
        for s in range(1, deep):
            low += lows[phase, s].astype(jnp.float32)
        ids = phase_ids(phase)
        scattered = jnp.concatenate(
            [jnp.where(ids == a, low, 0.0).astype(jnp.bfloat16) for a in range(count)], axis=0
        )
        for n in range(columns // TILE):
            cols = pl.ds(n * TILE, TILE)
            delta = lax.dot_general(
                scattered, up[:, :, cols].reshape(count * rank, TILE),
                (((0,), (0,)), ((), ())), preferred_element_type=jnp.float32,
            )
            total = base_out[phase, :, cols] + base_in[phase, :, cols] + adapter_scale * delta
            total = total.astype(jnp.bfloat16)
            for a in range(count):
                out_ref[pl.ds((a * phases + phase) * CHUNK, CHUNK), cols] = (
                    total[a * CHUNK:(a + 1) * CHUNK]
                )

    send_own(0)
    up_remote.start()
    for phase in range(phases):
        relay(phase, 1)
        pass_across(phase)
        if phase + 1 < phases:
            send_own(phase + 1)
        if phase == 1:
            down_copy.wait()
            w_copy.wait()
        if phase >= 1:
            project_down(phase - 1)
            project(phase - 1)
        for d in range(2, deep):
            relay(phase, d)
            if d == 2 and phase >= 1:
                share_low(phase - 1)
        if phase >= 1:
            spread_low(phase - 1)
        if phase == 1:
            up_copy.wait()
            up_remote.wait_recv()
        if phase >= 2:
            write(phase - 2)
        finish(phase)
    if phases == 1:
        down_copy.wait()
        w_copy.wait()
    last = phases - 1
    project_down(last)
    if last == 0:
        up_copy.wait()
        up_remote.wait_recv()
    share_low(last)
    project(last)
    spread_low(last)
    for phase in range(max(last - 1, 0), phases):
        write(phase)

    up_remote.wait_send()
    for phase in range(phases):
        part_copy(phase).wait_send()
        base_copy(phase).wait_send()
        if wide == 2:
            pair_copy(phase).wait_send()
        for k in range(1, deep):
            low_copy(phase, k).wait_send()
        for s in range(deep):
            when(jnp.logical_and(z >= s, z + 1 < deep),
                 lambda s=s: right(phase, s).wait_send())
            when(jnp.logical_and(z <= s, z > 0),
                 lambda s=s: left(phase, s).wait_send())
            if wide == 2:
                by_size(s, lambda size, s=s: side(phase, s, size).wait_send())
        if wide == 2:
            cross(phase, z).wait_send()


def local(count, wide, tokens, token_row_adapter, output_weight, down_weight, up_weight):
    own_rows, features = tokens.shape
    total_rows = token_row_adapter.shape[0]
    columns = output_weight.shape[1]
    rank = down_weight.shape[2]
    phases = own_rows // CHUNK
    deep = count // wide
    rows = count * CHUNK
    dma = pltpu.SemaphoreType.DMA
    hbm = pl.BlockSpec(memory_space=pltpu.HBM)
    vmem = pl.BlockSpec(memory_space=pltpu.VMEM)
    return pl.pallas_call(
        functools.partial(kernel, count, wide, phases),
        out_shape=jax.ShapeDtypeStruct((total_rows, columns), jnp.bfloat16),
        in_specs=[hbm, vmem, hbm, hbm, hbm],
        out_specs=vmem,
        scratch_shapes=[
            pltpu.VMEM((phases, rows, features), jnp.bfloat16),
            pltpu.VMEM((features, columns), jnp.bfloat16),
            pltpu.VMEM((rank, features), jnp.bfloat16),
            pltpu.VMEM((count, rank, columns), jnp.bfloat16),
            pltpu.VMEM((phases, rank, rows), jnp.float32),
            pltpu.VMEM((phases, rank, rows), jnp.float32),
            pltpu.VMEM((phases, rows, columns), jnp.float32),
            pltpu.VMEM((phases, rows, columns), jnp.float32),
            pltpu.VMEM((phases, 2, rank, rows), jnp.bfloat16),
            pltpu.VMEM((phases, deep, rank, rows), jnp.bfloat16),
            dma((3,)), dma((phases,)),
            dma, dma,
            dma((phases, deep)), dma((phases, deep)), dma((phases, deep)),
            dma((phases, deep)), dma((phases, deep)), dma((phases,)), dma((phases,)),
            dma((phases,)), dma((phases,)), dma((phases,)), dma((phases,)),
            dma((phases,)), dma((phases,)), dma((phases, deep)), dma((phases, deep)),
        ],
        compiler_params=pltpu.CompilerParams(
            collective_id=0, has_side_effects=True, vmem_limit_bytes=63 << 20
        ),
    )(tokens, token_row_adapter.reshape(1, total_rows), output_weight,
      jnp.swapaxes(down_weight, 1, 2), up_weight)


def solution(mesh):
    count = mesh.shape["adapter"]
    wide = 2 if count == 8 else 1
    placed = (
        P(("group", "adapter"), "tensor"),
        P("group", None),
        P("tensor", "adapter"),
        P(("group", "adapter"), "tensor", None),
        P("group", "tensor", "adapter"),
    )
    return jax.shard_map(
        functools.partial(local, count, wide),
        mesh=mesh, in_specs=placed, out_specs=P("group", "adapter"), check_vma=False,
    )
```

```python
import functools

import jax
import jax.numpy as jnp
from jax import lax
from jax.experimental import pallas as pl
from jax.experimental.pallas import tpu as pltpu
from jax.sharding import PartitionSpec as P

adapter_scale = 2.0
CHUNK = 16
PARTS = 2
TILE = 256
MESH = pl.DeviceIdType.MESH


def when(condition, action):
    pl.when(condition)(action)


def kernel(
    count, wide, phases,
    x_hbm, ids_ref, w_hbm, down_hbm, up_hbm, out_ref,
    xs, w, down, up, part_out, part_in, base_out, base_in, pair, lows,
    load_sem, own_sem,
    up_send, up_recv,
    right_send, left_send, line_recv,
    side_send, side_recv, cross_send, cross_recv,
    part_send, part_recv, base_send, base_recv, pair_send, pair_recv, low_send, low_recv,
):
    deep = count // wide
    me = lax.axis_index("adapter")
    core = lax.axis_index("tensor")
    z, y = lax.div(me, wide), lax.rem(me, wide)
    features = x_hbm.shape[1]
    width = features // PARTS
    rank = down.shape[0]
    half_rank = rank // 2
    columns = w.shape[1]
    rows = count * CHUNK
    beside = z + 1 - 2 * lax.rem(z, 2)
    mirror = 1 - y

    def place(zz, yy):
        return zz * wide + yy

    def block(phase, a, part):
        return xs.at[phase, pl.ds(pl.multiple_of(a * CHUNK, CHUNK), CHUNK),
                     pl.ds(part * width, width)]

    def own(phase, part):
        return x_hbm.at[pl.ds(phase * CHUNK, CHUNK), pl.ds(part * width, width)]

    def remote(src, dst, send, recv, **device):
        return pltpu.make_async_remote_copy(
            src_ref=src, dst_ref=dst, send_sem=send, recv_sem=recv,
            device_id=device, device_id_type=MESH,
        )

    w_copy = pltpu.make_async_copy(w_hbm, w, load_sem.at[0])
    down_copy = pltpu.make_async_copy(down_hbm.at[0], down, load_sem.at[1])
    up_rows = pl.ds(pl.multiple_of(core * half_rank, half_rank), half_rank)
    up_copy = pltpu.make_async_copy(up_hbm, up.at[:, up_rows, :], load_sem.at[2])
    up_remote = remote(up_hbm, up.at[:, up_rows, :], up_send, up_recv, tensor=1 - core)

    def own_copy(phase):
        return pltpu.make_async_copy(
            x_hbm.at[pl.ds(phase * CHUNK, CHUNK), :],
            xs.at[phase, pl.ds(pl.multiple_of(me * CHUNK, CHUNK), CHUNK), :],
            own_sem.at[phase],
        )

    w_copy.start()
    down_copy.start()
    up_copy.start()
    for phase in range(phases):
        own_copy(phase).start()

    barrier = pltpu.get_barrier_semaphore()
    pl.semaphore_signal(barrier, inc=1, device_id={"tensor": 1 - core}, device_id_type=MESH)
    for k in range(1, deep):
        pl.semaphore_signal(
            barrier, inc=1, device_id={"adapter": lax.rem(me + k * wide, count)},
            device_id_type=MESH,
        )
    if wide == 2:
        pl.semaphore_signal(
            barrier, inc=1, device_id={"adapter": place(z, mirror)}, device_id_type=MESH
        )
    pl.semaphore_wait(barrier, deep - 1 + wide)

    def right(phase, s, part, src=None):
        dst = block(phase, place(s, y), part)
        return remote(dst if src is None else src, dst, right_send.at[phase, s, part],
                      line_recv.at[phase, s, part], adapter=lax.rem(me + wide, count))

    def left(phase, s, part, src=None):
        dst = block(phase, place(s, y), part)
        return remote(dst if src is None else src, dst, left_send.at[phase, s, part],
                      line_recv.at[phase, s, part], adapter=lax.rem(me + count - wide, count))

    def side(phase, s, part, src=None):
        dst = block(phase, place(s, y), part)
        return remote(dst if src is None else src, dst, side_send.at[phase, s, part],
                      side_recv.at[phase, s, part], adapter=place(z, mirror))

    def side_in(phase, s, part):
        dst = block(phase, place(s, mirror), part)
        return remote(dst, dst, side_send.at[phase, s, part], side_recv.at[phase, s, part],
                      adapter=place(z, mirror))

    def cross(phase, s):
        dst = block(phase, place(s, mirror), PARTS - 1)
        return remote(dst, dst, cross_send.at[phase], cross_recv.at[phase],
                      adapter=place(beside, y))

    def unless_crossed(s, part, action):
        if part == PARTS - 1:
            when(s != beside, action)
        else:
            action()

    def send_own(phase):
        for part in range(PARTS):
            src = own(phase, part)
            when(z + 1 < deep, lambda: right(phase, z, part, src).start())
            when(z > 0, lambda: left(phase, z, part, src).start())
            if wide == 2:
                side(phase, z, part, src).start()

    def relay(phase, d):
        def pass_on(s, part):
            if wide == 2:
                unless_crossed(s, part, lambda: side(phase, s, part).start())

        def from_left(part):
            right(phase, z - d, part).wait_recv()
            when(z + 1 < deep, lambda: right(phase, z - d, part).start())
            pass_on(z - d, part)

        def from_right(part):
            left(phase, z + d, part).wait_recv()
            when(z > 0, lambda: left(phase, z + d, part).start())
            pass_on(z + d, part)

        for part in range(PARTS):
            when(z >= d, lambda: from_left(part))
            when(z + d < deep, lambda: from_right(part))

    def pass_across(phase):
        if wide == 2:
            for part in range(PARTS):
                side_in(phase, z, part).wait_recv()
            cross(phase, z).start()

    def finish(phase):
        own_copy(phase).wait()
        if wide == 2:
            for s in range(deep):
                for part in range(PARTS):
                    when(z != s, lambda: unless_crossed(
                        s, part, lambda: side_in(phase, s, part).wait_recv()))
            cross(phase, beside).wait_recv()

    def part_copy(phase):
        return remote(part_out.at[phase], part_in.at[phase], part_send.at[phase],
                      part_recv.at[phase], tensor=1 - core)

    def base_copy(phase):
        return remote(base_out.at[phase], base_in.at[phase], base_send.at[phase],
                      base_recv.at[phase], tensor=1 - core)

    def pair_copy(phase):
        return remote(pair.at[phase, 0], pair.at[phase, 1], pair_send.at[phase],
                      pair_recv.at[phase], adapter=place(z, mirror))

    def low_copy(phase, k):
        return remote(lows.at[phase, z], lows.at[phase, z], low_send.at[phase, k],
                      low_recv.at[phase, z], adapter=lax.rem(me + k * wide, count))

    def low_in(phase, k):
        source = lax.rem(z + k, deep)
        slot = lows.at[phase, source]
        return remote(slot, slot, low_send.at[phase, k], low_recv.at[phase, source],
                      adapter=place(source, y))

    def phase_ids(phase):
        return jnp.concatenate(
            [ids_ref[:, pl.ds((a * phases + phase) * CHUNK, CHUNK)] for a in range(count)], axis=1
        )

    def project_down(phase):
        low = lax.dot_general(
            down[...], xs[phase], (((1,), (1,)), ((), ())), preferred_element_type=jnp.float32
        )
        part_out[phase] = jnp.where(phase_ids(phase) == me, low, 0.0)
        part_copy(phase).start()

    def project(phase):
        @pl.loop(0, columns // TILE)
        def _(n):
            cols = pl.ds(pl.multiple_of(n * TILE, TILE), TILE)
            base_out[phase, :, cols] = jnp.dot(
                xs[phase], w[:, cols], preferred_element_type=jnp.float32
            )

        base_copy(phase).start()

    def share_low(phase):
        part_copy(phase).wait_recv()
        low = (part_out[phase] + part_in[phase]).astype(jnp.bfloat16)
        if wide == 2:
            pair[phase, 0] = low
            pair_copy(phase).start()
        else:
            lows[phase, z] = low

    def spread_low(phase):
        if wide == 2:
            pair_copy(phase).wait_recv()
            lows[phase, z] = pair[phase, 0] + pair[phase, 1]
        for k in range(1, deep):
            low_copy(phase, k).start()

    def write(phase):
        for k in range(1, deep):
            low_in(phase, k).wait_recv()
        base_copy(phase).wait_recv()
        low = lows[phase, 0].astype(jnp.float32)
        for s in range(1, deep):
            low += lows[phase, s].astype(jnp.float32)
        ids = phase_ids(phase)
        scattered = jnp.concatenate(
            [jnp.where(ids == a, low, 0.0) for a in range(count)], axis=0
        ).T.astype(jnp.bfloat16)
        for n in range(columns // TILE):
            cols = pl.ds(n * TILE, TILE)
            delta = jnp.dot(
                scattered, up[:, :, cols].reshape(count * rank, TILE),
                preferred_element_type=jnp.float32,
            )
            total = base_out[phase, :, cols] + base_in[phase, :, cols] + adapter_scale * delta
            total = total.astype(jnp.bfloat16)
            for a in range(count):
                out_ref[pl.ds((a * phases + phase) * CHUNK, CHUNK), cols] = (
                    total[a * CHUNK:(a + 1) * CHUNK]
                )

    send_own(0)
    up_remote.start()
    for phase in range(phases):
        relay(phase, 1)
        if phase + 1 < phases:
            pass_across(phase)
        if phase + 1 < phases:
            send_own(phase + 1)
        if phase == 1:
            down_copy.wait()
            w_copy.wait()
        if phase >= 1:
            finish(phase - 1)
            project_down(phase - 1)
            project(phase - 1)
        for d in range(2, deep):
            relay(phase, d)
            if d == 2 and phase >= 1:
                share_low(phase - 1)
        if phase + 1 == phases:
            pass_across(phase)
        if phase >= 1:
            spread_low(phase - 1)
        if phase == 1:
            up_copy.wait()
            up_remote.wait_recv()
        if phase >= 2:
            write(phase - 2)
    if phases == 1:
        down_copy.wait()
        w_copy.wait()
    last = phases - 1
    finish(last)
    project_down(last)
    if last == 0:
        up_copy.wait()
        up_remote.wait_recv()
    share_low(last)
    project(last)
    spread_low(last)
    for phase in range(max(last - 1, 0), phases):
        write(phase)

    up_remote.wait_send()
    for phase in range(phases):
        part_copy(phase).wait_send()
        base_copy(phase).wait_send()
        if wide == 2:
            pair_copy(phase).wait_send()
        for k in range(1, deep):
            low_copy(phase, k).wait_send()
        for s in range(deep):
            for part in range(PARTS):
                when(jnp.logical_and(z >= s, z + 1 < deep),
                     lambda: right(phase, s, part).wait_send())
                when(jnp.logical_and(z <= s, z > 0),
                     lambda: left(phase, s, part).wait_send())
                if wide == 2:
                    unless_crossed(s, part, lambda: side(phase, s, part).wait_send())
        if wide == 2:
            cross(phase, z).wait_send()


def local(count, wide, tokens, token_row_adapter, output_weight, down_weight, up_weight):
    own_rows, features = tokens.shape
    total_rows = token_row_adapter.shape[0]
    columns = output_weight.shape[1]
    rank = down_weight.shape[2]
    phases = own_rows // CHUNK
    deep = count // wide
    rows = count * CHUNK
    dma = pltpu.SemaphoreType.DMA
    hbm = pl.BlockSpec(memory_space=pltpu.HBM)
    vmem = pl.BlockSpec(memory_space=pltpu.VMEM)
    return pl.pallas_call(
        functools.partial(kernel, count, wide, phases),
        out_shape=jax.ShapeDtypeStruct((total_rows, columns), jnp.bfloat16),
        in_specs=[hbm, vmem, hbm, hbm, hbm],
        out_specs=vmem,
        scratch_shapes=[
            pltpu.VMEM((phases, rows, features), jnp.bfloat16),
            pltpu.VMEM((features, columns), jnp.bfloat16),
            pltpu.VMEM((rank, features), jnp.bfloat16),
            pltpu.VMEM((count, rank, columns), jnp.bfloat16),
            pltpu.VMEM((phases, rank, rows), jnp.float32),
            pltpu.VMEM((phases, rank, rows), jnp.float32),
            pltpu.VMEM((phases, rows, columns), jnp.float32),
            pltpu.VMEM((phases, rows, columns), jnp.float32),
            pltpu.VMEM((phases, 2, rank, rows), jnp.bfloat16),
            pltpu.VMEM((phases, deep, rank, rows), jnp.bfloat16),
            dma((3,)), dma((phases,)),
            dma, dma,
            *[dma((phases, deep, PARTS)) for _ in range(5)],
            dma((phases,)), dma((phases,)),
            dma((phases,)), dma((phases,)), dma((phases,)), dma((phases,)),
            dma((phases,)), dma((phases,)), dma((phases, deep)), dma((phases, deep)),
        ],
        compiler_params=pltpu.CompilerParams(
            collective_id=0, has_side_effects=True, vmem_limit_bytes=63 << 20
        ),
    )(tokens, token_row_adapter.reshape(1, total_rows), output_weight,
      jnp.swapaxes(down_weight, 1, 2), up_weight)


def solution(mesh):
    count = mesh.shape["adapter"]
    wide = 2 if count == 8 else 1
    placed = (
        P(("group", "adapter"), "tensor"),
        P("group", None),
        P("tensor", "adapter"),
        P(("group", "adapter"), "tensor", None),
        P("group", "tensor", "adapter"),
    )
    return jax.shard_map(
        functools.partial(local, count, wide),
        mesh=mesh, in_specs=placed, out_specs=P("group", "adapter"), check_vma=False,
    )
```
